512 devices in a mesh: tok: 8 (over y, core), voc: 16 (over z), tp: 4 (over x).
Axes of the slice: x: 4, y: 4, z: 16, core: 2. Of those that a mesh axis runs over, the one named last changes fastest.
Arguments:
- hidden: bfloat16 [512, 7168], P(('tok', 'voc'), 'tp'), may hold values from -8 to 8
- head_weight: bfloat16 [7168, 65536], P('tp', ('tok', 'voc')), may hold values from -1 to 1
- targets: int32 [512], replicated, may hold values from 0 to 65535
- offsets: int32 [32], replicated, may hold values from 1 to 511, as said below
- lengths: int32 [32], replicated, may hold values from 1 to 128
- group_ids: int32 [32], replicated, may hold values from 0 to 1, as said below
- rewards: float32 [32], replicated, may hold values from -4 to 4
Outputs:
- hidden_grad: bfloat16 [512, 7168], P(('tok', 'voc'), 'tp')
- policy_loss: float32 [], replicated
The draws below stay inside these ranges and needn't reach their ends.
Inputs may be any that keep to these rules, and one draw needn't show every extreme that they name: Rollouts lie packed in order over the 512 rows; the response of rollout i occupies rows offsets[i] to offsets[i] + lengths[i] - 1, ends that rollout and follows at least one prompt row of it; responses are disjoint and hold exactly 256 rows in all. `group_ids`: each of the 2 groups holds exactly 16 rollouts.
All inputs are finite; a program needn't handle non-finite values.
Results may differ from the reference program's by a relative error of at most 0.0054.
Values may be sent and summed in bfloat16 or wider, within the bound.
No kernel may reach another device: no remote copies, remote signals or barrier semaphores. Data moves between devices by JAX's collectives and lax.ppermute only.
A program may use at most 64 MiB of HBM per device.

```python
import math
import jax
import jax.numpy as jnp
from jax import lax

D = 7168
TOKENS = 512
ROLLOUTS = 32
GROUP_SIZE = 16
GROUPS = 2
VOCAB = 65536


def drawn_columns(key):
    column_key = jax.random.fold_in(key, 101)
    first_column = jax.random.randint(jax.random.fold_in(column_key, 1), (), 0, VOCAB)
    second_column = (first_column + 1 + jax.random.randint(jax.random.fold_in(column_key, 2), (), 0, VOCAB - 1)) % VOCAB
    signs = (jax.random.randint(jax.random.fold_in(column_key, 3), (D,), 0, 2) * 2 - 1).astype(jnp.float32)
    return (first_column, second_column, signs)


def column_level():
    return min(1.0, 8.0 / math.sqrt(D))


def cut_parts(key, whole, count):
    cuts = jnp.sort(jax.random.permutation(key, whole - 1)[:count - 1] + 1).astype(jnp.int32)
    bounds = jnp.concatenate([jnp.zeros((1,), jnp.int32), cuts, jnp.full((1,), whole, jnp.int32)])
    return bounds[1:] - bounds[:-1]


def rollout_layout(key):
    layout_key = jax.random.fold_in(key, 201)
    live_rows = TOKENS // 2
    longest = live_rows // 2
    prompts = cut_parts(jax.random.fold_in(layout_key, 1), live_rows, ROLLOUTS)
    others = cut_parts(jax.random.fold_in(layout_key, 2), live_rows - longest, ROLLOUTS - 1)
    planted = jax.random.randint(jax.random.fold_in(layout_key, 3), (), 0, ROLLOUTS)
    position = jnp.arange(ROLLOUTS, dtype=jnp.int32)
    source = jnp.clip(position - (position > planted).astype(jnp.int32), 0, ROLLOUTS - 2)
    response = jnp.where(position == planted, longest, jnp.take(others, source))
    spans = prompts + response
    ends = jnp.cumsum(spans).astype(jnp.int32)
    starts = ends - response
    return (starts.astype(jnp.int32), response.astype(jnp.int32))


def draw_hidden(key, part):
    first_column, second_column, signs = drawn_columns(key)
    key = jax.random.fold_in(key, 1)
    values = jnp.clip(jax.random.normal(key, (TOKENS, D), jnp.float32), -8.0, 8.0)
    row_index = jnp.arange(TOKENS, dtype=jnp.int32)[:, None]
    phase = row_index // 16 % 3
    target_score = jnp.where(phase == 0, 110.0, jnp.where(phase == 1, 170.0, 250.0))
    strength = target_score / (column_level() * D)
    values = jnp.where(row_index % 16 == 3, strength * signs[None, :], values)
    return values.astype(jnp.bfloat16)


def draw_head_weight(key, part):
    first_column, second_column, signs = drawn_columns(key)
    key = jax.random.fold_in(key, 2)
    spread = 3.0 / math.sqrt(D)
    values = jnp.clip(jax.random.normal(key, (D, VOCAB), jnp.float32) * spread, -1.0, 1.0)
    level = column_level()
    column_index = jnp.arange(VOCAB, dtype=jnp.int32)[None, :]
    values = jnp.where(column_index == first_column, signs[:, None] * level, values)
    values = jnp.where(column_index == second_column, signs[:, None] * (level * 0.99), values)
    return values.astype(jnp.bfloat16)


def draw_offsets(key, part):
    starts, response = rollout_layout(key)
    return starts


def draw_lengths(key, part):
    starts, response = rollout_layout(key)
    return response


def draw_group_ids(key, part):
    key = jax.random.fold_in(key, 5)
    order = jax.random.permutation(key, ROLLOUTS)
    return (order % GROUPS).astype(jnp.int32)


def touch_ends(entries, stream_key, smallest, top_value):
    place = [jax.random.randint(jax.random.fold_in(stream_key, axis), (), 0, length) for axis, length in enumerate(entries.shape)]
    widest = entries.shape.index(max(entries.shape))
    next_to = place[:widest] + [(place[widest] + 1) % entries.shape[widest]] + place[widest + 1:]
    return entries.at[tuple(place)].set(smallest).at[tuple(next_to)].set(top_value)


def centred(rng, dims, width, limit, kind=jnp.bfloat16):
    entries = jax.random.normal(rng, dims, jnp.float32) * width
    return jnp.minimum(jnp.maximum(entries, -limit), limit).astype(kind)


def setup_inputs(seed: int = 0) -> dict:
    key_list = jax.random.split(jax.random.key(seed), 8)
    return {
        "hidden": draw_hidden(jax.random.fold_in(key_list[7], 71), 0),
        "head_weight": draw_head_weight(jax.random.fold_in(key_list[7], 71), 0),
        "targets": touch_ends(jax.random.randint(key_list[2], (TOKENS,), 0, VOCAB), jax.random.fold_in(key_list[2], 1), 0, VOCAB - 1).astype(jnp.int32),
        "offsets": draw_offsets(jax.random.fold_in(key_list[7], 71), 0),
        "lengths": draw_lengths(jax.random.fold_in(key_list[7], 71), 0),
        "group_ids": draw_group_ids(jax.random.fold_in(key_list[7], 71), 0),
        "rewards": centred(key_list[6], (ROLLOUTS,), 1.0, 4.0, jnp.float32),
    }


entropy_weight = 0.2


def reference(hidden, head_weight, targets, offsets, lengths, group_ids, rewards):
    row_index = jnp.arange(TOKENS, dtype=jnp.int32)
    response_end = offsets + lengths
    member = ((row_index[:, None] >= offsets[None, :]) & (row_index[:, None] < response_end[None, :])).astype(jnp.float32)
    live_rows = jnp.sum(member, axis=1)
    grouping = (group_ids[:, None] == jnp.arange(GROUPS, dtype=jnp.int32)[None, :]).astype(jnp.float32)
    group_mean = jnp.sum(rewards[:, None] * grouping, axis=0) / GROUP_SIZE
    advantage = rewards - jnp.sum(grouping * group_mean[None, :], axis=1)
    row_advantage = jnp.sum(member * advantage[None, :], axis=1)
    weight_all = TOKENS / jnp.sum(lengths).astype(jnp.float32)
    logits = jnp.dot(hidden, head_weight, preferred_element_type=jnp.float32)
    row_top = jnp.max(logits, axis=1)
    shifted = jnp.exp(logits - row_top[:, None])
    total_exp = jnp.sum(shifted, axis=1)
    total_weighted = jnp.sum(shifted * logits, axis=1)
    log_total = row_top + jnp.log(total_exp)
    entropy = log_total - total_weighted / total_exp
    columns = jnp.arange(VOCAB, dtype=jnp.int32)
    target_hit = columns[None, :] == targets[:, None]
    target_value = jnp.sum(jnp.where(target_hit, logits, 0.0), axis=1)
    row_loss = live_rows * (-row_advantage * (target_value - log_total) - entropy_weight * entropy)
    policy_loss = weight_all * jnp.sum(row_loss)
    probability = jnp.exp(logits - log_total[:, None])
    row_weight = weight_all * live_rows
    grad_logits = row_weight[:, None] * (row_advantage[:, None] * (probability - target_hit.astype(jnp.float32)) + entropy_weight * probability * (logits - log_total[:, None] + entropy[:, None]))
    grad_logits = grad_logits.astype(jnp.bfloat16)
    hidden_grad = lax.dot_general(grad_logits, head_weight, (((1,), (1,)), ((), ())), preferred_element_type=jnp.float32)
    return hidden_grad.astype(jnp.bfloat16), policy_loss
```

```python
import jax
import jax.numpy as jnp
from jax import lax
from jax.sharding import Mesh, PartitionSpec as P

GROUP_SIZE = 16
GROUPS = 2
ENTROPY_WEIGHT = 0.2
Y, C, Z, X = 4, 2, 16, 4


def combine(stats):
    top = jnp.max(stats[:, 0], axis=0)
    scale = jnp.exp(stats[:, 0] - top[None])
    total = jnp.sum(scale * stats[:, 1], axis=0)
    weighted = jnp.sum(scale * (stats[:, 2] + (stats[:, 0] - top[None]) * stats[:, 1]), axis=0)
    target = jnp.sum(stats[:, 3], axis=0)
    return jnp.stack([top, total, weighted, target])


def spread(block, axes, n):
    sent = jnp.broadcast_to(block[None], (n, *block.shape))
    return lax.all_to_all(sent, axes, 0, 0, tiled=True)


def per_device(hidden, head_weight, targets, offsets, lengths, group_ids, rewards):
    y, c, z, x = (lax.axis_index(a) for a in ("y", "c", "z", "x"))
    depth, vocab = head_weight.shape
    total_rows = targets.shape[0]
    other_weight = lax.ppermute(head_weight, "c", [(0, 1), (1, 0)])

    rows = total_rows // C
    place = jnp.arange(rows, dtype=jnp.int32)
    per_tok = total_rows // (Y * C)
    row_index = (2 * (place // per_tok) + c) * per_tok + place % per_tok
    member = (
        (row_index[None, :] >= offsets[:, None])
        & (row_index[None, :] < (offsets + lengths)[:, None])
    ).astype(jnp.float32)
    live = jnp.sum(member, axis=0)
    grouping = (group_ids[:, None] == jnp.arange(GROUPS, dtype=jnp.int32)[None, :]).astype(jnp.float32)
    group_mean = jnp.sum(rewards[:, None] * grouping, axis=0) / GROUP_SIZE
    advantage = rewards - jnp.sum(grouping * group_mean[None, :], axis=1)
    row_advantage = jnp.sum(member * advantage[:, None], axis=0)
    weight_all = total_rows / jnp.sum(lengths).astype(jnp.float32)
    own_targets = targets.reshape(Y, C, per_tok)[:, c].reshape(rows)

    tok_rows = spread(hidden, "z", Z).reshape(per_tok, depth)
    my_rows = lax.all_gather(tok_rows, "y", axis=0, tiled=True)

    contract = (((0,), (1,)), ((), ()))
    part = jnp.concatenate(
        [
            lax.dot_general(w, my_rows, contract, preferred_element_type=jnp.float32)
            for w in (head_weight, other_weight)
        ]
    )
    chunk = C * vocab // X
    part = lax.all_to_all(part.reshape(X, chunk, rows), "x", 0, 0, tiled=True)
    logits = jnp.sum(part, axis=0)

    first = x * chunk
    core = jnp.where(first < vocab, c, 1 - c)
    first_column = ((2 * y + core) * Z + z) * vocab + first % vocab
    hit = (first_column + jnp.arange(chunk, dtype=jnp.int32))[:, None] == own_targets[None, :]
    top = jnp.max(logits, axis=0)
    shifted = logits - top[None]
    e = jnp.exp(shifted)
    stats = jnp.stack(
        [top, jnp.sum(e, 0), jnp.sum(e * shifted, 0), jnp.sum(jnp.where(hit, logits, 0.0), 0)]
    )
    stats = combine(spread(stats, "z", Z))
    top, total, weighted, target_value = combine(spread(stats, ("y", "x"), Y * X))
    log_sum = jnp.log(total)
    log_total = top + log_sum
    entropy = log_sum - weighted / total
    row_loss = live * (-row_advantage * (target_value - log_total) - ENTROPY_WEIGHT * entropy)
    loss = jnp.sum(row_loss)
    loss = weight_all * (loss + lax.ppermute(loss, "c", [(0, 1), (1, 0)]))

    log_probability = logits - log_total[None]
    probability = jnp.exp(log_probability)
    grad = (weight_all * live)[None] * (
        row_advantage[None] * (probability - hit.astype(jnp.float32))
        + ENTROPY_WEIGHT * probability * (log_probability + entropy[None])
    )
    grad = lax.all_gather(grad.astype(jnp.bfloat16), "x", axis=0, tiled=True)
    contract = (((0,), (1,)), ((), ()))
    hidden_grad = lax.dot_general(
        grad[:vocab], head_weight, contract, preferred_element_type=jnp.float32
    ) + lax.dot_general(grad[vocab:], other_weight, contract, preferred_element_type=jnp.float32)
    hidden_grad = hidden_grad.astype(jnp.bfloat16).reshape(Y, per_tok, depth)
    hidden_grad = lax.all_to_all(hidden_grad, "y", 0, 0, tiled=True)
    hidden_grad = jnp.sum(hidden_grad.astype(jnp.float32), axis=0).astype(jnp.bfloat16)
    hidden_grad = lax.all_to_all(hidden_grad.reshape(Z, per_tok // Z, depth), "z", 0, 0, tiled=True)
    hidden_grad = jnp.sum(hidden_grad.astype(jnp.float32), axis=0)
    return hidden_grad.astype(jnp.bfloat16), loss


def solution(mesh):
    split = Mesh(mesh.devices.reshape(Y, C, Z, X), ("y", "c", "z", "x"))
    voc = ("y", "c", "z")
    return jax.shard_map(
        per_device,
        mesh=split,
        in_specs=(P(voc, "x"), P("x", voc), P(), P(), P(), P(), P()),
        out_specs=(P(voc, "x"), P()),
        check_vma=False,
    )
```

```python
import jax
import jax.numpy as jnp
from jax import lax
from jax.experimental import pallas as pl
from jax.experimental.pallas import tpu as pltpu
from jax.sharding import Mesh, PartitionSpec as P

GROUP_SIZE = 16
GROUPS = 2
ENTROPY_WEIGHT = 0.2
Y, C, Z, X = 4, 2, 16, 4
VMEM = pl.BlockSpec(memory_space=pltpu.VMEM)
ANY = pl.BlockSpec(memory_space=pl.ANY)
PARAMS = pltpu.CompilerParams(vmem_limit_bytes=24 * 1024 * 1024)


def combine(stats):
    top = jnp.max(stats[:, 0], axis=0)
    scale = jnp.exp(stats[:, 0] - top[None])
    total = jnp.sum(scale * stats[:, 1], axis=0)
    weighted = jnp.sum(scale * (stats[:, 2] + (stats[:, 0] - top[None]) * stats[:, 1]), axis=0)
    target = jnp.sum(stats[:, 3], axis=0)
    return jnp.stack([top, total, weighted, target])


def spread(block, axes, n):
    sent = jnp.broadcast_to(block[None], (n, *block.shape))
    return lax.all_to_all(sent, axes, 0, 0, tiled=True)


def first_column(chunk, vocab, width):
    y, c, z = (lax.axis_index(a) for a in ("y", "c", "z"))
    per_core = vocab // width
    other = chunk // per_core
    core = c + other * (1 - 2 * c)
    return ((2 * y + core) * Z + z) * vocab + (chunk % per_core) * width


def logits_kernel(rows_ref, own_ref, other_hbm, out_ref, other_ref, sem):
    fetch = pltpu.make_async_copy(other_hbm, other_ref, sem)
    fetch.start()
    width = out_ref.shape[2]
    per_core = X // C
    for k in range(X):
        if k == per_core:
            fetch.wait()
        w_ref = own_ref if k < per_core else other_ref
        at = k % per_core * width
        out_ref[k] = jnp.dot(
            rows_ref[...], w_ref[:, at : at + width], preferred_element_type=jnp.float32
        )


def partial_logits(rows, own, other):
    n, depth = rows.shape
    vocab = own.shape[1]
    width = C * vocab // X
    return pl.pallas_call(
        logits_kernel,
        out_shape=jax.ShapeDtypeStruct((X, n, width), jnp.float32),
        in_specs=[VMEM, VMEM, ANY],
        out_specs=VMEM,
        scratch_shapes=[pltpu.VMEM(other.shape, other.dtype), pltpu.SemaphoreType.DMA],
        compiler_params=PARAMS,
        cost_estimate=pl.CostEstimate(
            flops=2 * n * depth * C * vocab, bytes_accessed=4 * X * n * width, transcendentals=0
        ),
        name="partial_logits",
    )(rows, own, other)


def stats_kernel(vocab, part_ref, target_ref, logits_ref, stats_ref):
    logits = part_ref[0] + part_ref[1] + part_ref[2] + part_ref[3]
    logits_ref[...] = logits
    n, width = logits.shape
    top = jnp.max(logits, axis=1, keepdims=True)
    shifted = logits - top
    e = jnp.exp(shifted)
    column = lax.broadcasted_iota(jnp.int32, (n, width), 1) + first_column(lax.axis_index("x"), vocab, width)
    hit = column == target_ref[...]
    values = (
        top,
        jnp.sum(e, axis=1, keepdims=True),
        jnp.sum(e * shifted, axis=1, keepdims=True),
        jnp.sum(jnp.where(hit, logits, 0.0), axis=1, keepdims=True),
    )
    lane = lax.broadcasted_iota(jnp.int32, (n, 128), 1)
    packed = jnp.zeros((n, 128), jnp.float32)
    for i, value in enumerate(values):
        packed = jnp.where(lane == i, value, packed)
    packed = packed.T[:8]
    for i in range(Z):
        stats_ref[i] = packed


def local_stats(part, target, vocab):
    _, n, width = part.shape
    return pl.pallas_call(
        lambda *refs: stats_kernel(vocab, *refs),
        out_shape=(
            jax.ShapeDtypeStruct((n, width), jnp.float32),
            jax.ShapeDtypeStruct((Z, 8, n), jnp.float32),
        ),
        in_specs=[VMEM, VMEM],
        out_specs=(VMEM, VMEM),
        compiler_params=PARAMS,
        cost_estimate=pl.CostEstimate(
            flops=8 * n * width, bytes_accessed=4 * X * n * width, transcendentals=n * width
        ),
        name="local_stats",
    )(part, target)


def grad_kernel(
    vocab, stats_ref, meta_ref, target_ref, l0, l1, l2, l3, own_ref, other_hbm, out_ref, loss_ref,
    g_ref, other_ref, sem
):
    fetch = pltpu.make_async_copy(other_hbm, other_ref, sem)
    fetch.start()
    tops = stats_ref[:, 0]
    top = jnp.max(tops, axis=0, keepdims=True)
    gap = tops - top
    scale = jnp.exp(gap)
    total = jnp.sum(scale * stats_ref[:, 1], axis=0, keepdims=True)
    weighted = jnp.sum(scale * (stats_ref[:, 2] + gap * stats_ref[:, 1]), axis=0, keepdims=True)
    target_value = jnp.sum(stats_ref[:, 3], axis=0, keepdims=True)
    log_sum = jnp.log(total)
    log_total = top + log_sum
    entropy = log_sum - weighted / total
    live, advantage, weight = meta_ref[0:1], meta_ref[1:2], meta_ref[2:3]
    row_loss = live * (-advantage * (target_value - log_total) - ENTROPY_WEIGHT * entropy)
    loss_ref[...] = jnp.sum(row_loss, axis=1, keepdims=True)

    n = live.shape[1]
    row = lax.broadcasted_iota(jnp.int32, (128, n), 0)
    packed = jnp.zeros((128, n), jnp.float32)
    for i, value in enumerate((log_total, entropy, weight * live, advantage)):
        packed = jnp.where(row == i, value, packed)
    packed = packed.T
    log_total, entropy, row_weight, advantage = (packed[:, i : i + 1] for i in range(4))
    width = l0.shape[1]
    x = lax.axis_index("x")
    target = target_ref[...]
    for k, l_ref in enumerate((l0, l1, l2, l3)):
        chunk = lax.rem(x + k, X)
        log_probability = l_ref[...] - log_total
        probability = jnp.exp(log_probability)
        column = lax.broadcasted_iota(jnp.int32, (n, width), 1) + first_column(chunk, vocab, width)
        hit = jnp.where(column == target, 1.0, 0.0)
        grad = row_weight * (
            advantage * (probability - hit)
            + ENTROPY_WEIGHT * probability * (log_probability + entropy)
        )
        g_ref[:, pl.ds(pl.multiple_of(chunk * width, width), width)] = grad.astype(jnp.bfloat16)
    contract = (((1,), (1,)), ((), ()))
    depth = own_ref.shape[0]
    step = 256
    fetch.wait()
    for at in range(0, depth, step):
        part = lax.dot_general(
            g_ref[:, :vocab], own_ref[at : at + step], contract, preferred_element_type=jnp.float32
        ) + lax.dot_general(
            g_ref[:, vocab:], other_ref[at : at + step], contract, preferred_element_type=jnp.float32
        )
        out_ref[:, at : at + step] = part.astype(jnp.bfloat16)


def partial_grad(stats, meta, target, chunks, own, other):
    n, width = chunks[0].shape
    depth, vocab = own.shape
    return pl.pallas_call(
        lambda *refs: grad_kernel(vocab, *refs),
        out_shape=(
            jax.ShapeDtypeStruct((n, depth), jnp.bfloat16),
            jax.ShapeDtypeStruct((1, 1), jnp.float32),
        ),
        in_specs=[VMEM] * 8 + [ANY],
        out_specs=(VMEM, VMEM),
        scratch_shapes=[
            pltpu.VMEM((n, C * vocab), jnp.bfloat16),
            pltpu.VMEM(other.shape, other.dtype),
            pltpu.SemaphoreType.DMA,
        ],
        compiler_params=PARAMS,
        cost_estimate=pl.CostEstimate(
            flops=2 * n * depth * C * vocab,
            bytes_accessed=4 * X * n * width,
            transcendentals=X * n * width,
        ),
        name="partial_grad",
    )(stats, meta, target, *chunks, own, other)


def per_device(hidden, head_weight, targets, offsets, lengths, group_ids, rewards):
    c = lax.axis_index("c")
    depth, vocab = head_weight.shape
    total_rows = targets.shape[0]

    rows = total_rows // C
    place = jnp.arange(rows, dtype=jnp.int32)
    per_tok = total_rows // (Y * C)
    row_index = (2 * (place // per_tok) + c) * per_tok + place % per_tok
    member = (
        (row_index[None, :] >= offsets[:, None])
        & (row_index[None, :] < (offsets + lengths)[:, None])
    ).astype(jnp.float32)
    live = jnp.sum(member, axis=0)
    grouping = (group_ids[:, None] == jnp.arange(GROUPS, dtype=jnp.int32)[None, :]).astype(jnp.float32)
    group_mean = jnp.sum(rewards[:, None] * grouping, axis=0) / GROUP_SIZE
    advantage = rewards - jnp.sum(grouping * group_mean[None, :], axis=1)
    row_advantage = jnp.sum(member * advantage[:, None], axis=0)
    weight_all = total_rows / jnp.sum(lengths).astype(jnp.float32)
    meta = jnp.stack([live, row_advantage, jnp.broadcast_to(weight_all, (rows,))])
    own_targets = targets.reshape(Y, C, per_tok)[:, c].reshape(rows, 1)

    swap = [(0, 1), (1, 0)]
    tok_rows = spread(hidden, "z", Z).reshape(per_tok, depth)
    other_weight = lax.ppermute(head_weight, "c", swap)
    tok_rows, meta, own_targets = lax.optimization_barrier((tok_rows, meta, own_targets))
    my_rows = lax.all_gather(tok_rows, "y", axis=0, tiled=True)

    part = partial_logits(my_rows, head_weight, other_weight)
    part = lax.all_to_all(part, "x", 0, 0, tiled=True)
    logits, stats = local_stats(part, own_targets, vocab)
    stats = lax.all_to_all(stats, "z", 0, 0, tiled=True)
    chunks = [logits] + [
        lax.ppermute(logits, "x", [((i + k) % X, i) for i in range(X)]) for k in range(1, X)
    ]
    stats = combine(stats[:, :4])
    stats = spread(stats, ("y", "x"), Y * X)
    hidden_grad, loss = partial_grad(stats, meta, own_targets, chunks, head_weight, other_weight)
    loss = loss[0, 0]

    hidden_grad = lax.all_to_all(hidden_grad.reshape(Y, per_tok, depth), "y", 0, 0, tiled=True)
    hidden_grad = jnp.sum(hidden_grad.astype(jnp.float32), axis=0).astype(jnp.bfloat16)
    hidden_grad = lax.all_to_all(hidden_grad.reshape(Z, per_tok // Z, depth), "z", 0, 0, tiled=True)
    hidden_grad = jnp.sum(hidden_grad.astype(jnp.float32), axis=0)
    loss = weight_all * (loss + lax.ppermute(loss, "c", swap))
    return hidden_grad.astype(jnp.bfloat16), loss


def solution(mesh):
    split = Mesh(mesh.devices.reshape(Y, C, Z, X), ("y", "c", "z", "x"))
    voc = ("y", "c", "z")
    return jax.shard_map(
        per_device,
        mesh=split,
        in_specs=(P(voc, "x"), P("x", voc), P(), P(), P(), P(), P()),
        out_specs=(P(voc, "x"), P()),
        check_vma=False,
    )
```

```python
import jax
import jax.numpy as jnp
from jax import lax
from jax.experimental import pallas as pl
from jax.experimental.pallas import tpu as pltpu
from jax.sharding import Mesh, PartitionSpec as P

GROUP_SIZE = 16
GROUPS = 2
ENTROPY_WEIGHT = 0.2
STEP = 256
Y, C, Z, X = 4, 2, 16, 4
VMEM = pl.BlockSpec(memory_space=pltpu.VMEM)
ANY = pl.BlockSpec(memory_space=pl.ANY)
PARAMS = pltpu.CompilerParams(vmem_limit_bytes=24 * 1024 * 1024)


def meta_kernel(offsets, lengths, groups, rewards, target_ref, out_ref):
    rollouts, rows = offsets.shape[0], out_ref.shape[1]
    per_tok = rows // Y
    place = lax.broadcasted_iota(jnp.int32, (1, rows), 1)
    row = (C * (place // per_tok) + lax.axis_index("c")) * per_tok + place % per_tok
    means = []
    for g in range(GROUPS):
        total = jnp.float32(0)
        for i in range(rollouts):
            total += jnp.where(groups[i] == g, rewards[i], jnp.float32(0))
        means.append(total / GROUP_SIZE)
    live = jnp.zeros((1, rows), jnp.float32)
    advantage = jnp.zeros((1, rows), jnp.float32)
    count = jnp.int32(0)
    for i in range(rollouts):
        first, length, mean = offsets[i], lengths[i], means[-1]
        for g in range(GROUPS - 1):
            mean = jnp.where(groups[i] == g, means[g], mean)
        member = jnp.where((row >= first) & (row < first + length), 1.0, 0.0)
        live += member
        advantage += member * (rewards[i] - mean)
        count += length
    weight = C * rows / jnp.full((1, rows), count, jnp.int32).astype(jnp.float32)
    out_ref[...] = jnp.concatenate(
        [live, advantage, weight, target_ref[...], jnp.zeros((4, rows), jnp.float32)], axis=0
    )


def row_meta(offsets, lengths, groups, rewards, target):
    smem = pl.BlockSpec(memory_space=pltpu.SMEM)
    return pl.pallas_call(
        meta_kernel,
        out_shape=jax.ShapeDtypeStruct((8, target.shape[1]), jnp.float32),
        in_specs=[smem] * 4 + [VMEM],
        out_specs=VMEM,
        compiler_params=PARAMS,
        name="row_meta",
    )(offsets, lengths, groups, rewards, target)


def merge(top, total, weighted, target):
    high = jnp.max(top, axis=0, keepdims=True)
    gap = top - high
    scale = jnp.exp(gap)
    return (
        high,
        jnp.sum(scale * total, axis=0, keepdims=True),
        jnp.sum(scale * (weighted + gap * total), axis=0, keepdims=True),
        jnp.sum(target, axis=0, keepdims=True),
    )


def merge_kernel(stats_ref, out_ref):
    parts = merge(*(stats_ref[:, i] for i in range(4)))
    block = jnp.concatenate([*parts, *parts], axis=0)
    for i in range(out_ref.shape[0]):
        out_ref[i] = block


def merged_stats(stats, copies):
    return pl.pallas_call(
        merge_kernel,
        out_shape=jax.ShapeDtypeStruct((copies, *stats.shape[1:]), jnp.float32),
        in_specs=[VMEM],
        out_specs=VMEM,
        compiler_params=PARAMS,
        name="merged_stats",
    )(stats)


def spread(block, axes, n):
    sent = jnp.broadcast_to(block[None], (n, *block.shape))
    return lax.all_to_all(sent, axes, 0, 0, tiled=True)


def x_neighbour(block, k):
    return lax.ppermute(block, "x", [((i + k) % X, i) for i in range(X)])


def first_column(chunk, vocab, width):
    y, c, z = (lax.axis_index(a) for a in ("y", "c", "z"))
    per_core = vocab // width
    other = chunk // per_core
    core = c + other * (1 - 2 * c)
    return ((2 * y + core) * Z + z) * vocab + (chunk % per_core) * width


def fetch_rows(parts, whole_ref, sem):
    size = parts[0].shape[0]
    copies = [
        pltpu.make_async_copy(part, whole_ref.at[i * size : (i + 1) * size], sem.at[i])
        for i, part in enumerate(parts)
    ]
    for copy in copies:
        copy.start()
    return copies


def logits_kernel(rows_ref, own_ref, *refs):
    *other_hbm, out_ref, other_ref, sem = refs
    fetch = fetch_rows(other_hbm, other_ref, sem)
    width = out_ref.shape[2]
    per_core = X // C
    for k in range(X):
        if k == per_core:
            for copy in fetch:
                copy.wait()
        w_ref = own_ref if k < per_core else other_ref
        at = k % per_core * width
        out_ref[k] = jnp.dot(
            rows_ref[...], w_ref[:, at : at + width], preferred_element_type=jnp.float32
        )


def partial_logits(rows, own, other):
    n, depth = rows.shape
    vocab = own.shape[1]
    width = C * vocab // X
    return pl.pallas_call(
        logits_kernel,
        out_shape=jax.ShapeDtypeStruct((X, n, width), jnp.float32),
        in_specs=[VMEM, VMEM] + [ANY] * len(other),
        out_specs=VMEM,
        scratch_shapes=[pltpu.VMEM(own.shape, own.dtype), pltpu.SemaphoreType.DMA((len(other),))],
        compiler_params=PARAMS,
        cost_estimate=pl.CostEstimate(
            flops=2 * n * depth * C * vocab, bytes_accessed=4 * X * n * width, transcendentals=0
        ),
        name="partial_logits",
    )(rows, own, *other)


def columns_of(values, n):
    row = lax.broadcasted_iota(jnp.int32, (128, n), 0)
    packed = jnp.zeros((128, n), jnp.float32)
    for i, value in enumerate(values):
        packed = jnp.where(row == i, value, packed)
    packed = packed.T
    return [packed[:, i : i + 1] for i in range(len(values))]


def stats_kernel(vocab, part_ref, meta_ref, logits_ref, stats_ref):
    logits = part_ref[0] + part_ref[1] + part_ref[2] + part_ref[3]
    logits_ref[...] = logits
    n, width = logits.shape
    top = jnp.max(logits, axis=1, keepdims=True)
    shifted = logits - top
    e = jnp.exp(shifted)
    column = lax.broadcasted_iota(jnp.int32, (n, width), 1) + first_column(lax.axis_index("x"), vocab, width)
    (target,) = columns_of([meta_ref[3:4, :n]], n)
    hit = column == target.astype(jnp.int32)
    values = (
        top,
        jnp.sum(e, axis=1, keepdims=True),
        jnp.sum(e * shifted, axis=1, keepdims=True),
        jnp.sum(jnp.where(hit, logits, 0.0), axis=1, keepdims=True),
    )
    lane = lax.broadcasted_iota(jnp.int32, (n, 128), 1)
    packed = jnp.zeros((n, 128), jnp.float32)
    for i, value in enumerate(values):
        packed = jnp.where(lane == i, value, packed)
    packed = packed.T[:8]
    for i in range(Z):
        stats_ref[i] = packed


def local_stats(part, meta, vocab):
    _, n, width = part.shape
    return pl.pallas_call(
        lambda *refs: stats_kernel(vocab, *refs),
        out_shape=(
            jax.ShapeDtypeStruct((n, width), jnp.float32),
            jax.ShapeDtypeStruct((Z, 8, n), jnp.float32),
        ),
        in_specs=[VMEM, VMEM],
        out_specs=(VMEM, VMEM),
        compiler_params=PARAMS,
        cost_estimate=pl.CostEstimate(
            flops=8 * n * width, bytes_accessed=4 * X * n * width, transcendentals=n * width
        ),
        name="local_stats",
    )(part, meta)


def grad_kernel(
    vocab, stats_ref, meta_ref, l0, l1, l2, l3, own_ref, *refs):
    *other_hbm, out_ref, loss_ref, g_ref, acc_ref, other_ref, sem = refs
    fetch = fetch_rows(other_hbm, other_ref, sem)
    n = l0.shape[0]
    top, total, weighted, target_value = merge(*(stats_ref[:, i] for i in range(4)))
    log_sum = jnp.log(total)
    log_total = top + log_sum
    entropy = log_sum - weighted / total
    live, advantage, weight, target = (meta_ref[i : i + 1] for i in range(4))
    row_loss = live * (-advantage * (target_value - log_total) - ENTROPY_WEIGHT * entropy)
    loss_ref[...] = weight[:, :1] * jnp.sum(row_loss, axis=1, keepdims=True)
    log_total, entropy, row_weight, advantage, target = columns_of(
        [log_total, entropy, weight * live, advantage, target], n
    )
    target = target.astype(jnp.int32)
    width = l0.shape[1]
    x = lax.axis_index("x")
    for k, l_ref in enumerate((l0, l1, l2, l3)):
        chunk = lax.rem(x + k, X)
        log_probability = l_ref[...] - log_total
        probability = jnp.exp(log_probability)
        column = lax.broadcasted_iota(jnp.int32, (n, width), 1) + first_column(chunk, vocab, width)
        hit = jnp.where(column == target, 1.0, 0.0)
        grad = row_weight * (
            advantage * (probability - hit)
            + ENTROPY_WEIGHT * probability * (log_probability + entropy)
        )
        g_ref[:, pl.ds(pl.multiple_of(chunk * width, width), width)] = grad.astype(jnp.bfloat16)
    contract = (((1,), (1,)), ((), ()))
    depth = own_ref.shape[0]
    for at in range(0, depth, STEP):
        acc_ref[:, at : at + STEP] = lax.dot_general(
            g_ref[:, :vocab], own_ref[at : at + STEP], contract, preferred_element_type=jnp.float32
        )
    for copy in fetch:
        copy.wait()
    for at in range(0, depth, STEP):
        part = acc_ref[:, at : at + STEP] + lax.dot_general(
            g_ref[:, vocab:], other_ref[at : at + STEP], contract, preferred_element_type=jnp.float32
        )
        out_ref[:, at : at + STEP] = part.astype(jnp.bfloat16)


def partial_grad(stats, meta, chunks, own, other):
    n, width = chunks[0].shape
    depth, vocab = own.shape
    return pl.pallas_call(
        lambda *refs: grad_kernel(vocab, *refs),
        out_shape=(
            jax.ShapeDtypeStruct((n, depth), jnp.bfloat16),
            jax.ShapeDtypeStruct((1, 1), jnp.float32),
        ),
        in_specs=[VMEM] * 7 + [ANY] * len(other),
        out_specs=(VMEM, VMEM),
        scratch_shapes=[
            pltpu.VMEM((n, C * vocab), jnp.bfloat16),
            pltpu.VMEM((n, depth), jnp.float32),
            pltpu.VMEM(own.shape, own.dtype),
            pltpu.SemaphoreType.DMA((len(other),)),
        ],
        compiler_params=PARAMS,
        cost_estimate=pl.CostEstimate(
            flops=2 * n * depth * C * vocab,
            bytes_accessed=4 * X * n * width,
            transcendentals=X * n * width,
        ),
        name="partial_grad",
    )(stats, meta, *chunks, own, *other)


def per_device(hidden, head_weight, targets, offsets, lengths, group_ids, rewards):
    c = lax.axis_index("c")
    depth, vocab = head_weight.shape
    total_rows = targets.shape[0]

    rows = total_rows // C
    per_tok = rows // Y
    own_targets = targets.astype(jnp.float32).reshape(Y, C, per_tok)[:, c].reshape(1, rows)
    meta = row_meta(offsets, lengths, group_ids, rewards, own_targets)

    swap = [(0, 1), (1, 0)]
    tok_rows = spread(hidden, "z", Z).reshape(per_tok, depth)
    other_weight = [lax.ppermute(w, "c", swap) for w in jnp.split(head_weight, 2)]
    tok_rows, meta = lax.optimization_barrier((tok_rows, meta))
    my_rows = lax.all_gather(tok_rows, "y", axis=0, tiled=True)

    part = partial_logits(my_rows, head_weight, other_weight)
    part = lax.all_to_all(part, "x", 0, 0, tiled=True)
    logits, stats = local_stats(part, meta, vocab)
    stats = lax.all_to_all(stats, "z", 0, 0, tiled=True)
    chunks = [logits, *(x_neighbour(logits, k) for k in range(1, X))]
    stats = lax.all_to_all(merged_stats(stats, Y * X), ("y", "x"), 0, 0, tiled=True)
    hidden_grad, loss = partial_grad(stats, meta, chunks, head_weight, other_weight)

    hidden_grad = lax.all_to_all(hidden_grad.reshape(Y, per_tok, depth), "y", 0, 0, tiled=True)
    hidden_grad = jnp.sum(hidden_grad.astype(jnp.float32), axis=0).astype(jnp.bfloat16)
    hidden_grad = lax.all_to_all(hidden_grad.reshape(Z, per_tok // Z, depth), "z", 0, 0, tiled=True)
    hidden_grad = jnp.sum(hidden_grad.astype(jnp.float32), axis=0)
    loss = loss[0, 0]
    return hidden_grad.astype(jnp.bfloat16), loss + lax.ppermute(loss, "c", swap)


def solution(mesh):
    split = Mesh(mesh.devices.reshape(Y, C, Z, X), ("y", "c", "z", "x"))
    voc = ("y", "c", "z")
    return jax.shard_map(
        per_device,
        mesh=split,
        in_specs=(P(voc, "x"), P("x", voc), P(), P(), P(), P(), P()),
        out_specs=(P(voc, "x"), P()),
        check_vma=False,
    )
```

```python
import jax
import jax.numpy as jnp
from jax import lax
from jax.experimental import pallas as pl
from jax.experimental.pallas import tpu as pltpu
from jax.sharding import Mesh, PartitionSpec as P

GROUP_SIZE = 16
GROUPS = 2
ENTROPY_WEIGHT = 0.2
STEP = 256
Y, C, Z, X = 4, 2, 16, 4
VMEM = pl.BlockSpec(memory_space=pltpu.VMEM)
ANY = pl.BlockSpec(memory_space=pl.ANY)
PARAMS = pltpu.CompilerParams(vmem_limit_bytes=24 * 1024 * 1024)


def meta_kernel(offsets, lengths, groups, rewards, target_ref, out_ref):
    rollouts, rows = offsets.shape[0], out_ref.shape[1]
    per_tok = rows // Y
    place = lax.broadcasted_iota(jnp.int32, (1, rows), 1)
    row = (C * (place // per_tok) + lax.axis_index("c")) * per_tok + place % per_tok
    means = []
    for g in range(GROUPS):
        total = jnp.float32(0)
        for i in range(rollouts):
            total += jnp.where(groups[i] == g, rewards[i], jnp.float32(0))
        means.append(total / GROUP_SIZE)
    live = jnp.zeros((1, rows), jnp.float32)
    advantage = jnp.zeros((1, rows), jnp.float32)
    count = jnp.int32(0)
    for i in range(rollouts):
        first, length, mean = offsets[i], lengths[i], means[-1]
        for g in range(GROUPS - 1):
            mean = jnp.where(groups[i] == g, means[g], mean)
        member = jnp.where((row >= first) & (row < first + length), 1.0, 0.0)
        live += member
        advantage += member * (rewards[i] - mean)
        count += length
    weight = C * rows / jnp.full((1, rows), count, jnp.int32).astype(jnp.float32)
    out_ref[...] = jnp.concatenate(
        [live, advantage, weight, target_ref[...], jnp.zeros((4, rows), jnp.float32)], axis=0
    )


def row_meta(offsets, lengths, groups, rewards, target):
    smem = pl.BlockSpec(memory_space=pltpu.SMEM)
    return pl.pallas_call(
        meta_kernel,
        out_shape=jax.ShapeDtypeStruct((8, target.shape[1]), jnp.float32),
        in_specs=[smem] * 4 + [VMEM],
        out_specs=VMEM,
        compiler_params=PARAMS,
        name="row_meta",
    )(offsets, lengths, groups, rewards, target)


def merge(top, total, weighted, target):
    high = jnp.max(top, axis=0, keepdims=True)
    gap = top - high
    scale = jnp.exp(gap)
    return (
        high,
        jnp.sum(scale * total, axis=0, keepdims=True),
        jnp.sum(scale * (weighted + gap * total), axis=0, keepdims=True),
        jnp.sum(target, axis=0, keepdims=True),
    )


def merge_kernel(stats_ref, out_ref):
    parts = merge(*(stats_ref[:, i] for i in range(4)))
    block = jnp.concatenate([*parts, *parts], axis=0)
    for i in range(out_ref.shape[0]):
        out_ref[i] = block


def merged_stats(stats, copies):
    return pl.pallas_call(
        merge_kernel,
        out_shape=jax.ShapeDtypeStruct((copies, *stats.shape[1:]), jnp.float32),
        in_specs=[VMEM],
        out_specs=VMEM,
        compiler_params=PARAMS,
        name="merged_stats",
    )(stats)


def spread(block, axes, n):
    sent = jnp.broadcast_to(block[None], (n, *block.shape))
    return lax.all_to_all(sent, axes, 0, 0, tiled=True)


def x_neighbour(block, k):
    return lax.ppermute(block, "x", [((i + k) % X, i) for i in range(X)])


def first_column(chunk, vocab, width):
    y, c, z = (lax.axis_index(a) for a in ("y", "c", "z"))
    per_core = vocab // width
    other = chunk // per_core
    core = c + other * (1 - 2 * c)
    return ((2 * y + core) * Z + z) * vocab + (chunk % per_core) * width


def fetch_rows(parts, whole_ref, sem):
    size = parts[0].shape[0]
    copies = [
        pltpu.make_async_copy(part, whole_ref.at[i * size : (i + 1) * size], sem.at[i])
        for i, part in enumerate(parts)
    ]
    for copy in copies:
        copy.start()
    return copies


def logits_kernel(rows_ref, own_ref, *refs):
    *other_hbm, out_ref, other_ref, sem = refs
    fetch = fetch_rows(other_hbm, other_ref, sem)
    width = out_ref.shape[2]
    per_core = X // C
    for k in range(X):
        if k == per_core:
            for copy in fetch:
                copy.wait()
        w_ref = own_ref if k < per_core else other_ref
        at = k % per_core * width
        out_ref[k] = jnp.dot(
            rows_ref[...], w_ref[:, at : at + width], preferred_element_type=jnp.float32
        )


def partial_logits(rows, own, other):
    n, depth = rows.shape
    vocab = own.shape[1]
    width = C * vocab // X
    return pl.pallas_call(
        logits_kernel,
        out_shape=jax.ShapeDtypeStruct((X, n, width), jnp.float32),
        in_specs=[VMEM, VMEM] + [ANY] * len(other),
        out_specs=VMEM,
        scratch_shapes=[pltpu.VMEM(own.shape, own.dtype), pltpu.SemaphoreType.DMA((len(other),))],
        compiler_params=PARAMS,
        cost_estimate=pl.CostEstimate(
            flops=2 * n * depth * C * vocab, bytes_accessed=4 * X * n * width, transcendentals=0
        ),
        name="partial_logits",
    )(rows, own, *other)


def columns_of(values, n):
    row = lax.broadcasted_iota(jnp.int32, (128, n), 0)
    packed = jnp.zeros((128, n), jnp.float32)
    for i, value in enumerate(values):
        packed = jnp.where(row == i, value, packed)
    packed = packed.T
    return [packed[:, i : i + 1] for i in range(len(values))]


def stats_kernel(vocab, part_ref, meta_ref, logits_ref, stats_ref):
    logits = part_ref[0] + part_ref[1] + part_ref[2] + part_ref[3]
    logits_ref[...] = logits
    n, width = logits.shape
    top = jnp.max(logits, axis=1, keepdims=True)
    shifted = logits - top
    e = jnp.exp(shifted)
    column = lax.broadcasted_iota(jnp.int32, (n, width), 1) + first_column(lax.axis_index("x"), vocab, width)
    (target,) = columns_of([meta_ref[3:4, :n]], n)
    hit = column == target.astype(jnp.int32)
    values = (
        top,
        jnp.sum(e, axis=1, keepdims=True),
        jnp.sum(e * shifted, axis=1, keepdims=True),
        jnp.sum(jnp.where(hit, logits, 0.0), axis=1, keepdims=True),
    )
    lane = lax.broadcasted_iota(jnp.int32, (n, 128), 1)
    packed = jnp.zeros((n, 128), jnp.float32)
    for i, value in enumerate(values):
        packed = jnp.where(lane == i, value, packed)
    packed = packed.T[:8]
    for i in range(Z):
        stats_ref[i] = packed


def local_stats(part, meta, vocab):
    _, n, width = part.shape
    return pl.pallas_call(
        lambda *refs: stats_kernel(vocab, *refs),
        out_shape=(
            jax.ShapeDtypeStruct((n, width), jnp.float32),
            jax.ShapeDtypeStruct((Z, 8, n), jnp.float32),
        ),
        in_specs=[VMEM, VMEM],
        out_specs=(VMEM, VMEM),
        compiler_params=PARAMS,
        cost_estimate=pl.CostEstimate(
            flops=8 * n * width, bytes_accessed=4 * X * n * width, transcendentals=n * width
        ),
        name="local_stats",
    )(part, meta)


def row_terms(stats_ref):
    top, total, weighted, target = merge(*(stats_ref[:, i] for i in range(4)))
    log_sum = jnp.log(total)
    return top + log_sum, log_sum - weighted / total, target


def loss_kernel(stats_ref, meta_ref, out_ref):
    log_total, entropy, target = row_terms(stats_ref)
    live, advantage, weight = (meta_ref[i : i + 1] for i in range(3))
    row_loss = live * (-advantage * (target - log_total) - ENTROPY_WEIGHT * entropy)
    out_ref[...] = weight[:, :1] * jnp.sum(row_loss, axis=1, keepdims=True)


def rows_loss(stats, meta):
    return pl.pallas_call(
        loss_kernel,
        out_shape=jax.ShapeDtypeStruct((1, 1), jnp.float32),
        in_specs=[VMEM, VMEM],
        out_specs=VMEM,
        compiler_params=PARAMS,
        name="rows_loss",
    )(stats, meta)


def grad_kernel(vocab, stats_ref, meta_ref, l0, l1, l2, l3, own_ref, *refs):
    *other_hbm, out_ref, g_ref, acc_ref, other_ref, l_ref, sem, move_sem = refs
    x = lax.axis_index("x")
    moves = [
        pltpu.make_async_copy(ref, l_ref.at[lax.rem(x + k, X)], move_sem.at[k])
        for k, ref in enumerate((l0, l1, l2, l3))
    ]
    for copy in moves:
        copy.start()
    fetch = fetch_rows(other_hbm, other_ref, sem)
    n = l0.shape[0]
    log_total, entropy, _ = row_terms(stats_ref)
    live, advantage, weight, target = (meta_ref[i : i + 1] for i in range(4))
    log_total, entropy, row_weight, advantage, target = columns_of(
        [log_total, entropy, weight * live, advantage, target], n
    )
    target = target.astype(jnp.int32)
    width = l0.shape[1]
    for copy in moves:
        copy.wait()
    for chunk in range(X):
        log_probability = l_ref[chunk] - log_total
        probability = jnp.exp(log_probability)
        column = lax.broadcasted_iota(jnp.int32, (n, width), 1) + first_column(chunk, vocab, width)
        hit = jnp.where(column == target, 1.0, 0.0)
        grad = row_weight * (
            advantage * (probability - hit)
            + ENTROPY_WEIGHT * probability * (log_probability + entropy)
        )
        g_ref[:, chunk * width : (chunk + 1) * width] = grad.astype(jnp.bfloat16)
    contract = (((1,), (1,)), ((), ()))
    depth = own_ref.shape[0]
    for at in range(0, depth, STEP):
        acc_ref[:, at : at + STEP] = lax.dot_general(
            g_ref[:, :vocab], own_ref[at : at + STEP], contract, preferred_element_type=jnp.float32
        )
    for copy in fetch:
        copy.wait()
    for at in range(0, depth, STEP):
        part = acc_ref[:, at : at + STEP] + lax.dot_general(
            g_ref[:, vocab:], other_ref[at : at + STEP], contract, preferred_element_type=jnp.float32
        )
        out_ref[:, at : at + STEP] = part.astype(jnp.bfloat16)


def partial_grad(stats, meta, chunks, own, other):
    n, width = chunks[0].shape
    depth, vocab = own.shape
    return pl.pallas_call(
        lambda *refs: grad_kernel(vocab, *refs),
        out_shape=jax.ShapeDtypeStruct((n, depth), jnp.bfloat16),
        in_specs=[VMEM] * 2 + [ANY] * X + [VMEM] + [ANY] * len(other),
        out_specs=VMEM,
        scratch_shapes=[
            pltpu.VMEM((n, C * vocab), jnp.bfloat16),
            pltpu.VMEM((n, depth), jnp.float32),
            pltpu.VMEM(own.shape, own.dtype),
            pltpu.VMEM((X, n, width), jnp.float32),
            pltpu.SemaphoreType.DMA((len(other),)),
            pltpu.SemaphoreType.DMA((X,)),
        ],
        compiler_params=PARAMS,
        cost_estimate=pl.CostEstimate(
            flops=2 * n * depth * C * vocab,
            bytes_accessed=4 * X * n * width,
            transcendentals=X * n * width,
        ),
        name="partial_grad",
    )(stats, meta, *chunks, own, *other)


def per_device(hidden, head_weight, targets, offsets, lengths, group_ids, rewards):
    c = lax.axis_index("c")
    depth, vocab = head_weight.shape
    total_rows = targets.shape[0]

    rows = total_rows // C
    per_tok = rows // Y
    own_targets = targets.astype(jnp.float32).reshape(Y, C, per_tok)[:, c].reshape(1, rows)
    meta = row_meta(offsets, lengths, group_ids, rewards, own_targets)

    swap = [(0, 1), (1, 0)]
    tok_rows = spread(hidden, "z", Z).reshape(per_tok, depth)
    other_weight = [lax.ppermute(w, "c", swap) for w in jnp.split(head_weight, 2)]
    tok_rows, meta = lax.optimization_barrier((tok_rows, meta))
    my_rows = lax.all_gather(tok_rows, "y", axis=0, tiled=True)

    part = partial_logits(my_rows, head_weight, other_weight)
    part = lax.all_to_all(part, "x", 0, 0, tiled=True)
    logits, stats = local_stats(part, meta, vocab)
    stats = lax.all_to_all(stats, "z", 0, 0, tiled=True)
    chunks = [logits, *(x_neighbour(logits, k) for k in range(1, X))]
    stats = lax.all_to_all(merged_stats(stats, Y * X), ("y", "x"), 0, 0, tiled=True)
    hidden_grad = partial_grad(stats, meta, chunks, head_weight, other_weight)

    hidden_grad = lax.all_to_all(hidden_grad.reshape(Y, per_tok, depth), "y", 0, 0, tiled=True)
    hidden_grad = jnp.sum(hidden_grad.astype(jnp.float32), axis=0).astype(jnp.bfloat16)
    hidden_grad = lax.all_to_all(hidden_grad.reshape(Z, per_tok // Z, depth), "z", 0, 0, tiled=True)
    hidden_grad = jnp.sum(hidden_grad.astype(jnp.float32), axis=0)
    loss = rows_loss(stats, meta)[0, 0]
    return hidden_grad.astype(jnp.bfloat16), loss + lax.ppermute(loss, "c", swap)


def solution(mesh):
    split = Mesh(mesh.devices.reshape(Y, C, Z, X), ("y", "c", "z", "x"))
    voc = ("y", "c", "z")
    return jax.shard_map(
        per_device,
        mesh=split,
        in_specs=(P(voc, "x"), P("x", voc), P(), P(), P(), P(), P()),
        out_specs=(P(voc, "x"), P()),
        check_vma=False,
    )
```

```python
import jax
import jax.numpy as jnp
from jax import lax
from jax.experimental import pallas as pl
from jax.experimental.pallas import tpu as pltpu
from jax.sharding import Mesh, PartitionSpec as P

GROUP_SIZE = 16
GROUPS = 2
ENTROPY_WEIGHT = 0.2
STEP = 256
Y, C, Z, X = 4, 2, 16, 4
VMEM = pl.BlockSpec(memory_space=pltpu.VMEM)
ANY = pl.BlockSpec(memory_space=pl.ANY)
PARAMS = pltpu.CompilerParams(vmem_limit_bytes=24 * 1024 * 1024)


def meta_kernel(offsets, lengths, groups, rewards, target_ref, out_ref):
    rollouts, rows = offsets.shape[0], out_ref.shape[1]
    per_tok = rows // Y
    place = lax.broadcasted_iota(jnp.int32, (1, rows), 1)
    row = (C * (place // per_tok) + lax.axis_index("c")) * per_tok + place % per_tok
    means = []
    for g in range(GROUPS):
        total = jnp.float32(0)
        for i in range(rollouts):
            total += jnp.where(groups[i] == g, rewards[i], jnp.float32(0))
        means.append(total / GROUP_SIZE)
    live = jnp.zeros((1, rows), jnp.float32)
    advantage = jnp.zeros((1, rows), jnp.float32)
    count = jnp.int32(0)
    for i in range(rollouts):
        first, length, mean = offsets[i], lengths[i], means[-1]
        for g in range(GROUPS - 1):
            mean = jnp.where(groups[i] == g, means[g], mean)
        member = jnp.where((row >= first) & (row < first + length), 1.0, 0.0)
        live += member
        advantage += member * (rewards[i] - mean)
        count += length
    weight = C * rows / jnp.full((1, rows), count, jnp.int32).astype(jnp.float32)
    out_ref[...] = jnp.concatenate(
        [live, advantage, weight, target_ref[...], jnp.zeros((4, rows), jnp.float32)], axis=0
    )


def row_meta(offsets, lengths, groups, rewards, target):
    smem = pl.BlockSpec(memory_space=pltpu.SMEM)
    return pl.pallas_call(
        meta_kernel,
        out_shape=jax.ShapeDtypeStruct((8, target.shape[1]), jnp.float32),
        in_specs=[smem] * 4 + [VMEM],
        out_specs=VMEM,
        compiler_params=PARAMS,
        name="row_meta",
    )(offsets, lengths, groups, rewards, target)


def merge(top, total, weighted, target):
    high = jnp.max(top, axis=0, keepdims=True)
    gap = top - high
    scale = jnp.exp(gap)
    return (
        high,
        jnp.sum(scale * total, axis=0, keepdims=True),
        jnp.sum(scale * (weighted + gap * total), axis=0, keepdims=True),
        jnp.sum(target, axis=0, keepdims=True),
    )


def fold(rows):
    half = rows.shape[1] // 2
    return jnp.concatenate([rows[:, :half], rows[:, half:]], axis=0)


def unfolded(stats_ref):
    return [jnp.concatenate([stats_ref[:, i], stats_ref[:, 4 + i]], axis=1) for i in range(4)]


def merge_kernel(stats_ref, out_ref):
    block = fold(jnp.concatenate(merge(*unfolded(stats_ref)), axis=0))
    for i in range(out_ref.shape[0]):
        out_ref[i] = block


def merged_stats(stats, copies):
    return pl.pallas_call(
        merge_kernel,
        out_shape=jax.ShapeDtypeStruct((copies, *stats.shape[1:]), jnp.float32),
        in_specs=[VMEM],
        out_specs=VMEM,
        compiler_params=PARAMS,
        name="merged_stats",
    )(stats)


def spread(block, axes, n):
    sent = jnp.broadcast_to(block[None], (n, *block.shape))
    return lax.all_to_all(sent, axes, 0, 0, tiled=True)


def x_neighbour(block, k):
    return lax.ppermute(block, "x", [((i + k) % X, i) for i in range(X)])


def first_column(chunk, vocab, width):
    y, c, z = (lax.axis_index(a) for a in ("y", "c", "z"))
    per_core = vocab // width
    other = chunk // per_core
    core = c + other * (1 - 2 * c)
    return ((2 * y + core) * Z + z) * vocab + (chunk % per_core) * width


def fetch_rows(parts, whole_ref, sem):
    size = parts[0].shape[0]
    copies = [
        pltpu.make_async_copy(part, whole_ref.at[i * size : (i + 1) * size], sem.at[i])
        for i, part in enumerate(parts)
    ]
    for copy in copies:
        copy.start()
    return copies


def logits_kernel(rows_ref, own_ref, *refs):
    *other_hbm, out_ref, other_ref, sem = refs
    fetch = fetch_rows(other_hbm, other_ref, sem)
    width = out_ref.shape[2]
    per_core = X // C
    for k in range(X):
        if k == per_core:
            for copy in fetch:
                copy.wait()
        w_ref = own_ref if k < per_core else other_ref
        at = k % per_core * width
        out_ref[k] = jnp.dot(
            rows_ref[...], w_ref[:, at : at + width], preferred_element_type=jnp.float32
        )


def partial_logits(rows, own, other):
    n, depth = rows.shape
    vocab = own.shape[1]
    width = C * vocab // X
    return pl.pallas_call(
        logits_kernel,
        out_shape=jax.ShapeDtypeStruct((X, n, width), jnp.float32),
        in_specs=[VMEM, VMEM] + [ANY] * len(other),
        out_specs=VMEM,
        scratch_shapes=[pltpu.VMEM(own.shape, own.dtype), pltpu.SemaphoreType.DMA((len(other),))],
        compiler_params=PARAMS,
        cost_estimate=pl.CostEstimate(
            flops=2 * n * depth * C * vocab, bytes_accessed=4 * X * n * width, transcendentals=0
        ),
        name="partial_logits",
    )(rows, own, *other)


def columns_of(values, n):
    row = lax.broadcasted_iota(jnp.int32, (128, n), 0)
    packed = jnp.zeros((128, n), jnp.float32)
    for i, value in enumerate(values):
        packed = jnp.where(row == i, value, packed)
    packed = packed.T
    return [packed[:, i : i + 1] for i in range(len(values))]


def stats_kernel(vocab, part_ref, meta_ref, logits_ref, stats_ref):
    logits = part_ref[0] + part_ref[1] + part_ref[2] + part_ref[3]
    logits_ref[...] = logits
    n, width = logits.shape
    top = jnp.max(logits, axis=1, keepdims=True)
    shifted = logits - top
    e = jnp.exp(shifted)
    column = lax.broadcasted_iota(jnp.int32, (n, width), 1) + first_column(lax.axis_index("x"), vocab, width)
    (target,) = columns_of([meta_ref[3:4, :n]], n)
    hit = column == target.astype(jnp.int32)
    values = (
        top,
        jnp.sum(e, axis=1, keepdims=True),
        jnp.sum(e * shifted, axis=1, keepdims=True),
        jnp.sum(jnp.where(hit, logits, 0.0), axis=1, keepdims=True),
    )
    lane = lax.broadcasted_iota(jnp.int32, (n, 128), 1)
    packed = jnp.zeros((n, 128), jnp.float32)
    for i, value in enumerate(values):
        packed = jnp.where(lane == i, value, packed)
    packed = fold(packed.T[:4])
    for i in range(Z):
        stats_ref[i] = packed


def local_stats(part, meta, vocab):
    _, n, width = part.shape
    return pl.pallas_call(
        lambda *refs: stats_kernel(vocab, *refs),
        out_shape=(
            jax.ShapeDtypeStruct((n, width), jnp.float32),
            jax.ShapeDtypeStruct((Z, 8, n // 2), jnp.float32),
        ),
        in_specs=[VMEM, VMEM],
        out_specs=(VMEM, VMEM),
        compiler_params=PARAMS,
        cost_estimate=pl.CostEstimate(
            flops=8 * n * width, bytes_accessed=4 * X * n * width, transcendentals=n * width
        ),
        name="local_stats",
    )(part, meta)


def row_terms(stats_ref):
    top, total, weighted, target = merge(*unfolded(stats_ref))
    log_sum = jnp.log(total)
    return top + log_sum, log_sum - weighted / total, target


def loss_kernel(stats_ref, meta_ref, out_ref):
    log_total, entropy, target = row_terms(stats_ref)
    live, advantage, weight = (meta_ref[i : i + 1] for i in range(3))
    row_loss = live * (-advantage * (target - log_total) - ENTROPY_WEIGHT * entropy)
    out_ref[...] = weight[:, :1] * jnp.sum(row_loss, axis=1, keepdims=True)


def rows_loss(stats, meta):
    return pl.pallas_call(
        loss_kernel,
        out_shape=jax.ShapeDtypeStruct((1, 1), jnp.float32),
        in_specs=[VMEM, VMEM],
        out_specs=VMEM,
        compiler_params=PARAMS,
        name="rows_loss",
    )(stats, meta)


def grad_kernel(vocab, stats_ref, meta_ref, l0, l1, l2, l3, own_ref, *refs):
    *other_hbm, out_ref, g_ref, acc_ref, other_ref, l_ref, sem, move_sem = refs
    x = lax.axis_index("x")
    moves = [
        pltpu.make_async_copy(ref, l_ref.at[lax.rem(x + k, X)], move_sem.at[k])
        for k, ref in enumerate((l0, l1, l2, l3))
    ]
    for copy in moves:
        copy.start()
    fetch = fetch_rows(other_hbm, other_ref, sem)
    n = l0.shape[0]
    log_total, entropy, _ = row_terms(stats_ref)
    live, advantage, weight, target = (meta_ref[i : i + 1] for i in range(4))
    log_total, entropy, row_weight, advantage, target = columns_of(
        [log_total, entropy, weight * live, advantage, target], n
    )
    target = target.astype(jnp.int32)
    width = l0.shape[1]
    for copy in moves:
        copy.wait()
    for chunk in range(X):
        log_probability = l_ref[chunk] - log_total
        probability = jnp.exp(log_probability)
        column = lax.broadcasted_iota(jnp.int32, (n, width), 1) + first_column(chunk, vocab, width)
        hit = jnp.where(column == target, 1.0, 0.0)
        grad = row_weight * (
            advantage * (probability - hit)
            + ENTROPY_WEIGHT * probability * (log_probability + entropy)
        )
        g_ref[:, chunk * width : (chunk + 1) * width] = grad.astype(jnp.bfloat16)
    contract = (((1,), (1,)), ((), ()))
    depth = own_ref.shape[0]
    for at in range(0, depth, STEP):
        acc_ref[:, at : at + STEP] = lax.dot_general(
            g_ref[:, :vocab], own_ref[at : at + STEP], contract, preferred_element_type=jnp.float32
        )
    for copy in fetch:
        copy.wait()
    for at in range(0, depth, STEP):
        part = acc_ref[:, at : at + STEP] + lax.dot_general(
            g_ref[:, vocab:], other_ref[at : at + STEP], contract, preferred_element_type=jnp.float32
        )
        out_ref[:, at : at + STEP] = part.astype(jnp.bfloat16)


def partial_grad(stats, meta, chunks, own, other):
    n, width = chunks[0].shape
    depth, vocab = own.shape
    return pl.pallas_call(
        lambda *refs: grad_kernel(vocab, *refs),
        out_shape=jax.ShapeDtypeStruct((n, depth), jnp.bfloat16),
        in_specs=[VMEM] * 2 + [ANY] * X + [VMEM] + [ANY] * len(other),
        out_specs=VMEM,
        scratch_shapes=[
            pltpu.VMEM((n, C * vocab), jnp.bfloat16),
            pltpu.VMEM((n, depth), jnp.float32),
            pltpu.VMEM(own.shape, own.dtype),
            pltpu.VMEM((X, n, width), jnp.float32),
            pltpu.SemaphoreType.DMA((len(other),)),
            pltpu.SemaphoreType.DMA((X,)),
        ],
        compiler_params=PARAMS,
        cost_estimate=pl.CostEstimate(
            flops=2 * n * depth * C * vocab,
            bytes_accessed=4 * X * n * width,
            transcendentals=X * n * width,
        ),
        name="partial_grad",
    )(stats, meta, *chunks, own, *other)


def per_device(hidden, head_weight, targets, offsets, lengths, group_ids, rewards):
    c = lax.axis_index("c")
    depth, vocab = head_weight.shape
    total_rows = targets.shape[0]

    rows = total_rows // C
    per_tok = rows // Y
    own_targets = targets.astype(jnp.float32).reshape(Y, C, per_tok)[:, c].reshape(1, rows)
    meta = row_meta(offsets, lengths, group_ids, rewards, own_targets)

    swap = [(0, 1), (1, 0)]
    tok_rows = spread(hidden, "z", Z).reshape(per_tok, depth)
    other_weight = [lax.ppermute(w, "c", swap) for w in jnp.split(head_weight, 2)]
    tok_rows, meta = lax.optimization_barrier((tok_rows, meta))
    my_rows = lax.all_gather(tok_rows, "y", axis=0, tiled=True)

    part = partial_logits(my_rows, head_weight, other_weight)
    part = lax.all_to_all(part, "x", 0, 0, tiled=True)
    logits, stats = local_stats(part, meta, vocab)
    stats = lax.all_to_all(stats, "z", 0, 0, tiled=True)
    chunks = [logits, *(x_neighbour(logits, k) for k in range(1, X))]
    stats = lax.all_to_all(merged_stats(stats, Y * X), ("y", "x"), 0, 0, tiled=True)
    hidden_grad = partial_grad(stats, meta, chunks, head_weight, other_weight)

    hidden_grad = lax.all_to_all(hidden_grad.reshape(Y, per_tok, depth), "y", 0, 0, tiled=True)
    hidden_grad = jnp.sum(hidden_grad.astype(jnp.float32), axis=0).astype(jnp.bfloat16)
    hidden_grad = lax.all_to_all(hidden_grad.reshape(Z, per_tok // Z, depth), "z", 0, 0, tiled=True)
    hidden_grad = jnp.sum(hidden_grad.astype(jnp.float32), axis=0)
    loss = rows_loss(stats, meta)[0, 0]
    return hidden_grad.astype(jnp.bfloat16), loss + lax.ppermute(loss, "c", swap)


def solution(mesh):
    split = Mesh(mesh.devices.reshape(Y, C, Z, X), ("y", "c", "z", "x"))
    voc = ("y", "c", "z")
    return jax.shard_map(
        per_device,
        mesh=split,
        in_specs=(P(voc, "x"), P("x", voc), P(), P(), P(), P(), P()),
        out_specs=(P(voc, "x"), P()),
        check_vma=False,
    )
```

```python
import jax
import jax.numpy as jnp
from jax import lax
from jax.experimental import pallas as pl
from jax.experimental.pallas import tpu as pltpu
from jax.sharding import Mesh, PartitionSpec as P

GROUP_SIZE = 16
GROUPS = 2
ENTROPY_WEIGHT = 0.2
STEP = 256
Y, C, Z, X = 4, 2, 16, 4
VMEM = pl.BlockSpec(memory_space=pltpu.VMEM)
ANY = pl.BlockSpec(memory_space=pl.ANY)
PARAMS = pltpu.CompilerParams(vmem_limit_bytes=24 * 1024 * 1024)


def meta_kernel(offsets, lengths, groups, rewards, target_ref, out_ref):
    rollouts, rows = offsets.shape[0], out_ref.shape[1]
    per_tok = rows // Y
    place = lax.broadcasted_iota(jnp.int32, (1, rows), 1)
    row = (C * (place // per_tok) + lax.axis_index("c")) * per_tok + place % per_tok
    means = []
    for g in range(GROUPS):
        total = jnp.float32(0)
        for i in range(rollouts):
            total += jnp.where(groups[i] == g, rewards[i], jnp.float32(0))
        means.append(total / GROUP_SIZE)
    live = jnp.zeros((1, rows), jnp.float32)
    advantage = jnp.zeros((1, rows), jnp.float32)
    count = jnp.int32(0)
    for i in range(rollouts):
        first, length, mean = offsets[i], lengths[i], means[-1]
        for g in range(GROUPS - 1):
            mean = jnp.where(groups[i] == g, means[g], mean)
        member = jnp.where((row >= first) & (row < first + length), 1.0, 0.0)
        live += member
        advantage += member * (rewards[i] - mean)
        count += length
    weight = C * rows / jnp.full((1, rows), count, jnp.int32).astype(jnp.float32)
    out_ref[...] = jnp.concatenate(
        [live, advantage, weight, target_ref[...], jnp.zeros((4, rows), jnp.float32)], axis=0
    )


def row_meta(offsets, lengths, groups, rewards, target):
    smem = pl.BlockSpec(memory_space=pltpu.SMEM)
    return pl.pallas_call(
        meta_kernel,
        out_shape=jax.ShapeDtypeStruct((8, target.shape[1]), jnp.float32),
        in_specs=[smem] * 4 + [VMEM],
        out_specs=VMEM,
        compiler_params=PARAMS,
        name="row_meta",
    )(offsets, lengths, groups, rewards, target)


def merge(top, total, weighted, target):
    high = jnp.max(top, axis=0, keepdims=True)
    gap = top - high
    scale = jnp.exp(gap)
    return (
        high,
        jnp.sum(scale * total, axis=0, keepdims=True),
        jnp.sum(scale * (weighted + gap * total), axis=0, keepdims=True),
        jnp.sum(target, axis=0, keepdims=True),
    )


def fold(rows):
    half = rows.shape[1] // 2
    return jnp.concatenate([rows[:, :half], rows[:, half:]], axis=0)


def unfolded(stats_ref):
    return [jnp.concatenate([stats_ref[:, i], stats_ref[:, 4 + i]], axis=1) for i in range(4)]


def merge_kernel(stats_ref, out_ref):
    block = fold(jnp.concatenate(merge(*unfolded(stats_ref)), axis=0))
    for i in range(out_ref.shape[0]):
        out_ref[i] = block


def merged_stats(stats, copies):
    return pl.pallas_call(
        merge_kernel,
        out_shape=jax.ShapeDtypeStruct((copies, *stats.shape[1:]), jnp.float32),
        in_specs=[VMEM],
        out_specs=VMEM,
        compiler_params=PARAMS,
        name="merged_stats",
    )(stats)


def spread(block, axes, n):
    sent = jnp.broadcast_to(block[None], (n, *block.shape))
    return lax.all_to_all(sent, axes, 0, 0, tiled=True)


def x_neighbour(block, k):
    return lax.ppermute(block, "x", [((i + k) % X, i) for i in range(X)])


def first_column(chunk, vocab, width):
    y, c, z = (lax.axis_index(a) for a in ("y", "c", "z"))
    per_core = vocab // width
    other = chunk // per_core
    core = c + other * (1 - 2 * c)
    return ((2 * y + core) * Z + z) * vocab + (chunk % per_core) * width


def fetch_rows(parts, whole_ref, sem):
    size = parts[0].shape[0]
    copies = [
        pltpu.make_async_copy(part, whole_ref.at[i * size : (i + 1) * size], sem.at[i])
        for i, part in enumerate(parts)
    ]
    for copy in copies:
        copy.start()
    return copies


def logits_kernel(rows_ref, own_ref, *refs):
    *other_hbm, out_ref, other_ref, sem = refs
    fetch = fetch_rows(other_hbm, other_ref, sem)
    width = out_ref.shape[2]
    per_core = X // C
    for k in range(X):
        if k == per_core:
            for copy in fetch:
                copy.wait()
        w_ref = own_ref if k < per_core else other_ref
        at = k % per_core * width
        out_ref[k] = jnp.dot(
            rows_ref[...], w_ref[:, at : at + width], preferred_element_type=jnp.float32
        )


def partial_logits(rows, own, other):
    n, depth = rows.shape
    vocab = own.shape[1]
    width = C * vocab // X
    return pl.pallas_call(
        logits_kernel,
        out_shape=jax.ShapeDtypeStruct((X, n, width), jnp.float32),
        in_specs=[VMEM, VMEM] + [ANY] * len(other),
        out_specs=VMEM,
        scratch_shapes=[pltpu.VMEM(own.shape, own.dtype), pltpu.SemaphoreType.DMA((len(other),))],
        compiler_params=PARAMS,
        cost_estimate=pl.CostEstimate(
            flops=2 * n * depth * C * vocab, bytes_accessed=4 * X * n * width, transcendentals=0
        ),
        name="partial_logits",
    )(rows, own, *other)


def columns_of(values, n):
    row = lax.broadcasted_iota(jnp.int32, (128, n), 0)
    packed = jnp.zeros((128, n), jnp.float32)
    for i, value in enumerate(values):
        packed = jnp.where(row == i, value, packed)
    packed = packed.T
    return [packed[:, i : i + 1] for i in range(len(values))]


def stats_kernel(vocab, part_ref, meta_ref, logits_ref, stats_ref):
    logits = part_ref[0] + part_ref[1] + part_ref[2] + part_ref[3]
    logits_ref[...] = logits
    n, width = logits.shape
    top = jnp.max(logits, axis=1, keepdims=True)
    shifted = logits - top
    e = jnp.exp(shifted)
    column = lax.broadcasted_iota(jnp.int32, (n, width), 1) + first_column(lax.axis_index("x"), vocab, width)
    (target,) = columns_of([meta_ref[3:4, :n]], n)
    hit = column == target.astype(jnp.int32)
    values = (
        top,
        jnp.sum(e, axis=1, keepdims=True),
        jnp.sum(e * shifted, axis=1, keepdims=True),
        jnp.sum(jnp.where(hit, logits, 0.0), axis=1, keepdims=True),
    )
    lane = lax.broadcasted_iota(jnp.int32, (n, 128), 1)
    packed = jnp.zeros((n, 128), jnp.float32)
    for i, value in enumerate(values):
        packed = jnp.where(lane == i, value, packed)
    packed = fold(packed.T[:4])
    for i in range(stats_ref.shape[0]):
        stats_ref[i] = packed


def local_stats(part, meta, vocab):
    _, n, width = part.shape
    return pl.pallas_call(
        lambda *refs: stats_kernel(vocab, *refs),
        out_shape=(
            jax.ShapeDtypeStruct((n, width), jnp.float32),
            jax.ShapeDtypeStruct((Y * X, 8, n // 2), jnp.float32),
        ),
        in_specs=[VMEM, VMEM],
        out_specs=(VMEM, VMEM),
        compiler_params=PARAMS,
        cost_estimate=pl.CostEstimate(
            flops=8 * n * width, bytes_accessed=4 * X * n * width, transcendentals=n * width
        ),
        name="local_stats",
    )(part, meta)


def row_terms(stats_ref):
    top, total, weighted, target = merge(*unfolded(stats_ref))
    log_sum = jnp.log(total)
    return top + log_sum, log_sum - weighted / total, target


def loss_kernel(stats_ref, meta_ref, out_ref):
    log_total, entropy, target = row_terms(stats_ref)
    live, advantage, weight = (meta_ref[i : i + 1] for i in range(3))
    row_loss = live * (-advantage * (target - log_total) - ENTROPY_WEIGHT * entropy)
    out_ref[...] = weight[:, :1] * jnp.sum(row_loss, axis=1, keepdims=True)


def rows_loss(stats, meta):
    return pl.pallas_call(
        loss_kernel,
        out_shape=jax.ShapeDtypeStruct((1, 1), jnp.float32),
        in_specs=[VMEM, VMEM],
        out_specs=VMEM,
        compiler_params=PARAMS,
        name="rows_loss",
    )(stats, meta)


def grad_kernel(vocab, stats_ref, meta_ref, l0, l1, l2, l3, own_ref, *refs):
    *other_hbm, out_ref, g_ref, acc_ref, other_ref, l_ref, sem, move_sem = refs
    x = lax.axis_index("x")
    moves = [
        pltpu.make_async_copy(ref, l_ref.at[lax.rem(x + k, X)], move_sem.at[k])
        for k, ref in enumerate((l0, l1, l2, l3))
    ]
    for copy in moves:
        copy.start()
    fetch = fetch_rows(other_hbm, other_ref, sem)
    n = l0.shape[0]
    log_total, entropy, _ = row_terms(stats_ref)
    live, advantage, weight, target = (meta_ref[i : i + 1] for i in range(4))
    log_total, entropy, row_weight, advantage, target = columns_of(
        [log_total, entropy, weight * live, advantage, target], n
    )
    target = target.astype(jnp.int32)
    width = l0.shape[1]
    for copy in moves:
        copy.wait()
    for chunk in range(X):
        log_probability = l_ref[chunk] - log_total
        probability = jnp.exp(log_probability)
        column = lax.broadcasted_iota(jnp.int32, (n, width), 1) + first_column(chunk, vocab, width)
        hit = jnp.where(column == target, 1.0, 0.0)
        grad = row_weight * (
            advantage * (probability - hit)
            + ENTROPY_WEIGHT * probability * (log_probability + entropy)
        )
        g_ref[:, chunk * width : (chunk + 1) * width] = grad.astype(jnp.bfloat16)
    contract = (((1,), (1,)), ((), ()))
    depth = own_ref.shape[0]
    for at in range(0, depth, STEP):
        acc_ref[:, at : at + STEP] = lax.dot_general(
            g_ref[:, :vocab], own_ref[at : at + STEP], contract, preferred_element_type=jnp.float32
        )
    for copy in fetch:
        copy.wait()
    for at in range(0, depth, STEP):
        part = acc_ref[:, at : at + STEP] + lax.dot_general(
            g_ref[:, vocab:], other_ref[at : at + STEP], contract, preferred_element_type=jnp.float32
        )
        out_ref[:, at : at + STEP] = part.astype(jnp.bfloat16)


def partial_grad(stats, meta, chunks, own, other):
    n, width = chunks[0].shape
    depth, vocab = own.shape
    return pl.pallas_call(
        lambda *refs: grad_kernel(vocab, *refs),
        out_shape=jax.ShapeDtypeStruct((n, depth), jnp.bfloat16),
        in_specs=[VMEM] * 2 + [ANY] * X + [VMEM] + [ANY] * len(other),
        out_specs=VMEM,
        scratch_shapes=[
            pltpu.VMEM((n, C * vocab), jnp.bfloat16),
            pltpu.VMEM((n, depth), jnp.float32),
            pltpu.VMEM(own.shape, own.dtype),
            pltpu.VMEM((X, n, width), jnp.float32),
            pltpu.SemaphoreType.DMA((len(other),)),
            pltpu.SemaphoreType.DMA((X,)),
        ],
        compiler_params=PARAMS,
        cost_estimate=pl.CostEstimate(
            flops=2 * n * depth * C * vocab,
            bytes_accessed=4 * X * n * width,
            transcendentals=X * n * width,
        ),
        name="partial_grad",
    )(stats, meta, *chunks, own, *other)


def per_device(hidden, head_weight, targets, offsets, lengths, group_ids, rewards):
    c = lax.axis_index("c")
    depth, vocab = head_weight.shape
    total_rows = targets.shape[0]

    rows = total_rows // C
    per_tok = rows // Y
    own_targets = targets.astype(jnp.float32).reshape(Y, C, per_tok)[:, c].reshape(1, rows)
    meta = row_meta(offsets, lengths, group_ids, rewards, own_targets)

    swap = [(0, 1), (1, 0)]
    tok_rows = spread(hidden, "z", Z).reshape(per_tok, depth)
    other_weight = [lax.ppermute(w, "c", swap) for w in jnp.split(head_weight, 2)]
    tok_rows, meta = lax.optimization_barrier((tok_rows, meta))
    my_rows = lax.all_gather(tok_rows, "y", axis=0, tiled=True)

    part = partial_logits(my_rows, head_weight, other_weight)
    part = lax.all_to_all(part, "x", 0, 0, tiled=True)
    logits, stats = local_stats(part, meta, vocab)
    stats = lax.all_to_all(stats, ("y", "x"), 0, 0, tiled=True)
    chunks = [logits, *(x_neighbour(logits, k) for k in range(1, X))]
    stats = lax.all_to_all(merged_stats(stats, Z), "z", 0, 0, tiled=True)
    hidden_grad = partial_grad(stats, meta, chunks, head_weight, other_weight)

    hidden_grad = lax.all_to_all(hidden_grad.reshape(Y, per_tok, depth), "y", 0, 0, tiled=True)
    hidden_grad = jnp.sum(hidden_grad.astype(jnp.float32), axis=0).astype(jnp.bfloat16)
    hidden_grad = lax.all_to_all(hidden_grad.reshape(Z, per_tok // Z, depth), "z", 0, 0, tiled=True)
    hidden_grad = jnp.sum(hidden_grad.astype(jnp.float32), axis=0)
    loss = rows_loss(stats, meta)[0, 0]
    return hidden_grad.astype(jnp.bfloat16), loss + lax.ppermute(loss, "c", swap)


def solution(mesh):
    split = Mesh(mesh.devices.reshape(Y, C, Z, X), ("y", "c", "z", "x"))
    voc = ("y", "c", "z")
    return jax.shard_map(
        per_device,
        mesh=split,
        in_specs=(P(voc, "x"), P("x", voc), P(), P(), P(), P(), P()),
        out_specs=(P(voc, "x"), P()),
        check_vma=False,
    )
```

```python
import jax
import jax.numpy as jnp
from jax import lax
from jax.experimental import pallas as pl
from jax.experimental.pallas import tpu as pltpu
from jax.sharding import Mesh, PartitionSpec as P

GROUP_SIZE = 16
GROUPS = 2
ENTROPY_WEIGHT = 0.2
Y, C, Z, X = 4, 2, 16, 4
VMEM = pl.BlockSpec(memory_space=pltpu.VMEM)
ANY = pl.BlockSpec(memory_space=pl.ANY)
PARAMS = pltpu.CompilerParams(vmem_limit_bytes=24 * 1024 * 1024)


def meta_kernel(offsets, lengths, groups, rewards, target_ref, out_ref):
    rollouts, rows = offsets.shape[0], out_ref.shape[1]
    per_tok = rows // Y
    place = lax.broadcasted_iota(jnp.int32, (1, rows), 1)
    row = (C * (place // per_tok) + lax.axis_index("c")) * per_tok + place % per_tok
    means = []
    for g in range(GROUPS):
        total = jnp.float32(0)
        for i in range(rollouts):
            total += jnp.where(groups[i] == g, rewards[i], jnp.float32(0))
        means.append(total / GROUP_SIZE)
    live = jnp.zeros((1, rows), jnp.float32)
    advantage = jnp.zeros((1, rows), jnp.float32)
    count = jnp.int32(0)
    for i in range(rollouts):
        first, length, mean = offsets[i], lengths[i], means[-1]
        for g in range(GROUPS - 1):
            mean = jnp.where(groups[i] == g, means[g], mean)
        member = jnp.where((row >= first) & (row < first + length), 1.0, 0.0)
        live += member
        advantage += member * (rewards[i] - mean)
        count += length
    weight = C * rows / jnp.full((1, rows), count, jnp.int32).astype(jnp.float32)
    out_ref[...] = jnp.concatenate(
        [live, advantage, weight, target_ref[...], jnp.zeros((4, rows), jnp.float32)], axis=0
    )


def row_meta(offsets, lengths, groups, rewards, target):
    smem = pl.BlockSpec(memory_space=pltpu.SMEM)
    return pl.pallas_call(
        meta_kernel,
        out_shape=jax.ShapeDtypeStruct((8, target.shape[1]), jnp.float32),
        in_specs=[smem] * 4 + [VMEM],
        out_specs=VMEM,
        compiler_params=PARAMS,
        name="row_meta",
    )(offsets, lengths, groups, rewards, target)


def merge(top, total, weighted, target):
    high = jnp.max(top, axis=0, keepdims=True)
    gap = top - high
    scale = jnp.exp(gap)
    return (
        high,
        jnp.sum(scale * total, axis=0, keepdims=True),
        jnp.sum(scale * (weighted + gap * total), axis=0, keepdims=True),
        jnp.sum(target, axis=0, keepdims=True),
    )


def fold(rows):
    half = rows.shape[1] // 2
    return jnp.concatenate([rows[:, :half], rows[:, half:]], axis=0)


def unfolded(stats_ref):
    return [jnp.concatenate([stats_ref[:, i], stats_ref[:, 4 + i]], axis=1) for i in range(4)]


def merge_kernel(stats_ref, out_ref):
    block = fold(jnp.concatenate(merge(*unfolded(stats_ref)), axis=0))
    for i in range(out_ref.shape[0]):
        out_ref[i] = block


def merged_stats(stats, copies):
    return pl.pallas_call(
        merge_kernel,
        out_shape=jax.ShapeDtypeStruct((copies, *stats.shape[1:]), jnp.float32),
        in_specs=[VMEM],
        out_specs=VMEM,
        compiler_params=PARAMS,
        name="merged_stats",
    )(stats)


def spread(block, axes, n):
    sent = jnp.broadcast_to(block[None], (n, *block.shape))
    return lax.all_to_all(sent, axes, 0, 0, tiled=True)


def x_neighbour(block, k):
    return lax.ppermute(block, "x", [((i + k) % X, i) for i in range(X)])


def first_column(chunk, vocab, width):
    y, c, z = (lax.axis_index(a) for a in ("y", "c", "z"))
    per_core = vocab // width
    other = chunk // per_core
    core = c + other * (1 - 2 * c)
    return ((2 * y + core) * Z + z) * vocab + (chunk % per_core) * width


def fetch_rows(parts, whole_ref, sem):
    size = parts[0].shape[0]
    copies = [
        pltpu.make_async_copy(part, whole_ref.at[i * size : (i + 1) * size], sem.at[i])
        for i, part in enumerate(parts)
    ]
    for copy in copies:
        copy.start()
    return copies


def logits_kernel(rows_ref, own_ref, *refs):
    *other_hbm, out_ref, other_ref, sem = refs
    fetch = fetch_rows(other_hbm, other_ref, sem)
    width = out_ref.shape[2]
    per_core = X // C
    for k in range(X):
        if k == per_core:
            for copy in fetch:
                copy.wait()
        w_ref = own_ref if k < per_core else other_ref
        at = k % per_core * width
        out_ref[k] = jnp.dot(
            rows_ref[...], w_ref[:, at : at + width], preferred_element_type=jnp.float32
        )


def partial_logits(rows, own, other):
    n, depth = rows.shape
    vocab = own.shape[1]
    width = C * vocab // X
    return pl.pallas_call(
        logits_kernel,
        out_shape=jax.ShapeDtypeStruct((X, n, width), jnp.float32),
        in_specs=[VMEM, VMEM] + [ANY] * len(other),
        out_specs=VMEM,
        scratch_shapes=[pltpu.VMEM(own.shape, own.dtype), pltpu.SemaphoreType.DMA((len(other),))],
        compiler_params=PARAMS,
        cost_estimate=pl.CostEstimate(
            flops=2 * n * depth * C * vocab, bytes_accessed=4 * X * n * width, transcendentals=0
        ),
        name="partial_logits",
    )(rows, own, *other)


def columns_of(values, n):
    row = lax.broadcasted_iota(jnp.int32, (128, n), 0)
    packed = jnp.zeros((128, n), jnp.float32)
    for i, value in enumerate(values):
        packed = jnp.where(row == i, value, packed)
    packed = packed.T
    return [packed[:, i : i + 1] for i in range(len(values))]


def stats_kernel(vocab, part_ref, meta_ref, logits_ref, stats_ref):
    logits = part_ref[0] + part_ref[1] + part_ref[2] + part_ref[3]
    logits_ref[...] = logits
    n, width = logits.shape
    top = jnp.max(logits, axis=1, keepdims=True)
    shifted = logits - top
    e = jnp.exp(shifted)
    column = lax.broadcasted_iota(jnp.int32, (n, width), 1) + first_column(lax.axis_index("x"), vocab, width)
    (target,) = columns_of([meta_ref[3:4, :n]], n)
    hit = column == target.astype(jnp.int32)
    values = (
        top,
        jnp.sum(e, axis=1, keepdims=True),
        jnp.sum(e * shifted, axis=1, keepdims=True),
        jnp.sum(jnp.where(hit, logits, 0.0), axis=1, keepdims=True),
    )
    lane = lax.broadcasted_iota(jnp.int32, (n, 128), 1)
    packed = jnp.zeros((n, 128), jnp.float32)
    for i, value in enumerate(values):
        packed = jnp.where(lane == i, value, packed)
    packed = fold(packed.T[:4])
    for i in range(stats_ref.shape[0]):
        stats_ref[i] = packed


def local_stats(part, meta, vocab):
    _, n, width = part.shape
    return pl.pallas_call(
        lambda *refs: stats_kernel(vocab, *refs),
        out_shape=(
            jax.ShapeDtypeStruct((n, width), jnp.float32),
            jax.ShapeDtypeStruct((Y * X, 8, n // 2), jnp.float32),
        ),
        in_specs=[VMEM, VMEM],
        out_specs=(VMEM, VMEM),
        compiler_params=PARAMS,
        cost_estimate=pl.CostEstimate(
            flops=8 * n * width, bytes_accessed=4 * X * n * width, transcendentals=n * width
        ),
        name="local_stats",
    )(part, meta)


def row_terms(stats_ref):
    top, total, weighted, target = merge(*unfolded(stats_ref))
    log_sum = jnp.log(total)
    return top + log_sum, log_sum - weighted / total, target


def loss_kernel(stats_ref, meta_ref, out_ref):
    log_total, entropy, target = row_terms(stats_ref)
    live, advantage, weight = (meta_ref[i : i + 1] for i in range(3))
    row_loss = live * (-advantage * (target - log_total) - ENTROPY_WEIGHT * entropy)
    out_ref[...] = weight[:, :1] * jnp.sum(row_loss, axis=1, keepdims=True)


def rows_loss(stats, meta):
    return pl.pallas_call(
        loss_kernel,
        out_shape=jax.ShapeDtypeStruct((1, 1), jnp.float32),
        in_specs=[VMEM, VMEM],
        out_specs=VMEM,
        compiler_params=PARAMS,
        name="rows_loss",
    )(stats, meta)


def grad_kernel(vocab, stats_ref, meta_ref, l0, l1, l2, l3, own_ref, *refs):
    *other_hbm, out_ref, other_ref, l_ref, sem, move_sem = refs
    x = lax.axis_index("x")
    moves = [
        pltpu.make_async_copy(ref, l_ref.at[lax.rem(x + k, X)], move_sem.at[k])
        for k, ref in enumerate((l0, l1, l2, l3))
    ]
    for copy in moves:
        copy.start()
    fetch = fetch_rows(other_hbm, other_ref, sem)
    n = l0.shape[0]
    log_total, entropy, _ = row_terms(stats_ref)
    live, advantage, weight, target = (meta_ref[i : i + 1] for i in range(4))
    log_total, entropy, row_weight, advantage, target = columns_of(
        [log_total, entropy, weight * live, advantage, target], n
    )
    target = target.astype(jnp.int32)
    width = l0.shape[1]
    for copy in moves:
        copy.wait()

    def core_grad(first):
        parts = []
        for chunk in range(first, first + X // C):
            log_probability = l_ref[chunk] - log_total
            probability = jnp.exp(log_probability)
            column = lax.broadcasted_iota(jnp.int32, (n, width), 1) + first_column(chunk, vocab, width)
            hit = jnp.where(column == target, 1.0, 0.0)
            grad = row_weight * (
                advantage * (probability - hit)
                + ENTROPY_WEIGHT * probability * (log_probability + entropy)
            )
            parts.append(grad.astype(jnp.bfloat16))
        return jnp.concatenate(parts, axis=1)

    contract = (((1,), (1,)), ((), ()))
    own = lax.dot_general(core_grad(0), own_ref[...], contract, preferred_element_type=jnp.float32)
    for copy in fetch:
        copy.wait()
    other = lax.dot_general(core_grad(X // C), other_ref[...], contract, preferred_element_type=jnp.float32)
    out_ref[...] = (own + other).astype(jnp.bfloat16)


def partial_grad(stats, meta, chunks, own, other):
    n, width = chunks[0].shape
    depth, vocab = own.shape
    return pl.pallas_call(
        lambda *refs: grad_kernel(vocab, *refs),
        out_shape=jax.ShapeDtypeStruct((n, depth), jnp.bfloat16),
        in_specs=[VMEM] * 2 + [ANY] * X + [VMEM] + [ANY] * len(other),
        out_specs=VMEM,
        scratch_shapes=[
            pltpu.VMEM(own.shape, own.dtype),
            pltpu.VMEM((X, n, width), jnp.float32),
            pltpu.SemaphoreType.DMA((len(other),)),
            pltpu.SemaphoreType.DMA((X,)),
        ],
        compiler_params=PARAMS,
        cost_estimate=pl.CostEstimate(
            flops=2 * n * depth * C * vocab,
            bytes_accessed=4 * X * n * width,
            transcendentals=X * n * width,
        ),
        name="partial_grad",
    )(stats, meta, *chunks, own, *other)


def per_device(hidden, head_weight, targets, offsets, lengths, group_ids, rewards):
    c = lax.axis_index("c")
    depth, vocab = head_weight.shape
    total_rows = targets.shape[0]

    rows = total_rows // C
    per_tok = rows // Y
    own_targets = targets.astype(jnp.float32).reshape(Y, C, per_tok)[:, c].reshape(1, rows)
    meta = row_meta(offsets, lengths, group_ids, rewards, own_targets)

    swap = [(0, 1), (1, 0)]
    tok_rows = spread(hidden, "z", Z).reshape(per_tok, depth)
    other_weight = [lax.ppermute(w, "c", swap) for w in jnp.split(head_weight, 2)]
    tok_rows, meta = lax.optimization_barrier((tok_rows, meta))
    my_rows = lax.all_gather(tok_rows, "y", axis=0, tiled=True)

    part = partial_logits(my_rows, head_weight, other_weight)
    part = lax.all_to_all(part, "x", 0, 0, tiled=True)
    logits, stats = local_stats(part, meta, vocab)
    stats = lax.all_to_all(stats, ("y", "x"), 0, 0, tiled=True)
    chunks = [logits, *(x_neighbour(logits, k) for k in range(1, X))]
    stats = lax.all_to_all(merged_stats(stats, Z), "z", 0, 0, tiled=True)
    hidden_grad = partial_grad(stats, meta, chunks, head_weight, other_weight)

    hidden_grad = lax.all_to_all(hidden_grad.reshape(Y, per_tok, depth), "y", 0, 0, tiled=True)
    hidden_grad = jnp.sum(hidden_grad.astype(jnp.float32), axis=0).astype(jnp.bfloat16)
    hidden_grad = lax.all_to_all(hidden_grad.reshape(Z, per_tok // Z, depth), "z", 0, 0, tiled=True)
    hidden_grad = jnp.sum(hidden_grad.astype(jnp.float32), axis=0)
    loss = rows_loss(stats, meta)[0, 0]
    return hidden_grad.astype(jnp.bfloat16), loss + lax.ppermute(loss, "c", swap)


def solution(mesh):
    split = Mesh(mesh.devices.reshape(Y, C, Z, X), ("y", "c", "z", "x"))
    voc = ("y", "c", "z")
    return jax.shard_map(
        per_device,
        mesh=split,
        in_specs=(P(voc, "x"), P("x", voc), P(), P(), P(), P(), P()),
        out_specs=(P(voc, "x"), P()),
        check_vma=False,
    )
```
